32 devices in a mesh: rows: 8 (over z, x), cols: 4 (over y, core).
Axes of the slice: x: 2, y: 2, z: 4, core: 2. Of those that a mesh axis runs over, the one named last changes fastest.
Arguments:
- hankel: float32 [256, 32768], P('rows', 'cols'), may hold values from -6 to 6
- shifted: float32 [256, 32768], P('rows', 'cols'), may hold values from -6 to 6
- start_basis: float32 [32768, 128], P(('cols', 'rows')), may hold values from -0.03125 to 0.03125
Outputs:
- basis: float32 [256, 128], P('rows')
- operator: float32 [128, 128], replicated
The draws below stay inside these ranges and needn't reach their ends.
All inputs are finite; a program needn't handle non-finite values.
Results may differ from the reference program's by a relative error of at most 0.0002.
Values sent between devices are 32-bit elements; how exact they have to be, the bound alone decides.
A program may use at most 64 MiB of HBM per device.

```python
import math
import jax
import jax.numpy as jnp
from jax import lax

S = 32768
K = 128
P_SIZE = 256


def with_spikes(drawn, key, source, target, blocks, factor):
    owner, partner = [(jnp.arange(drawn.shape[dim]) // (drawn.shape[dim] // blocks)).reshape([-1 if axis == dim else 1 for axis in range(drawn.ndim)]) for dim in (source, target)]
    chosen = jax.random.permutation(key, blocks)[partner]
    strong = (owner == chosen) | (owner == (partner + blocks // 2) % blocks)
    return jnp.where(strong, factor * drawn, drawn)


def level_of(stream_key, dims, cuts, low, high):
    def one(dim, shards_of):
        draws = jax.random.uniform(jax.random.fold_in(jax.random.fold_in(stream_key, 6), dim), (shards_of,), jnp.float32, low / len(cuts), high / len(cuts))
        return jnp.repeat(jnp.exp(draws), dims[dim] // shards_of).reshape((-1,) + (1,) * (len(dims) - dim - 1))

    factor_of = one(*cuts[0])
    for cut in cuts[1:]:
        factor_of = factor_of * one(*cut)
    return factor_of


def centred(key, shape, spread, reach, shards=(), kind=jnp.bfloat16):
    array = jax.random.normal(key, shape, jnp.float32) * spread
    if len(shards) > 0:
        array = level_of(key, shape, shards, -0.22, 0.18) * array
    return jnp.clip(array, min=-reach, max=reach).astype(kind)


def gaussian_with(rng, extent, spread, bound, shards, heavy, dtype=jnp.bfloat16):
    drawn = spread * jax.random.normal(rng, extent, jnp.float32)
    if shards:
        drawn = drawn * level_of(rng, extent, shards, -0.22, 0.18)
    return jnp.clip(with_spikes(drawn, jax.random.fold_in(rng, 3), *heavy), -bound, bound).astype(dtype)


def setup_inputs(seed: int = 0) -> dict:
    arg_keys = jax.random.split(jax.random.key(seed), 4)
    hankel = gaussian_with(arg_keys[0], (P_SIZE, S), 1.0, 6.0, ((0, 8), (1, 4)), (0, 1, 8, 2.0), jnp.float32)
    shifted = centred(arg_keys[1], (P_SIZE, S), 1.0, 6.0, ((0, 8), (1, 4)), jnp.float32)
    start_basis = centred(arg_keys[2], (S, K), S ** -0.5, 0.03125, ((0, 32),), jnp.float32)
    return {"hankel": hankel, "shifted": shifted, "start_basis": start_basis}


def product(left, right):
    return jnp.dot(left.astype(jnp.float32), right.astype(jnp.float32), precision=lax.Precision.HIGHEST, preferred_element_type=jnp.float32)

def right_solve(values, lower):
    return lax.linalg.triangular_solve(lower, values, left_side=False, lower=True, transpose_a=True)

def orthonormal(columns, total):
    gram = product(columns.T, columns) / total
    lower = jnp.linalg.cholesky(gram)
    return right_solve(columns, lower)

def reference(hankel, shifted, start_basis):
    total = hankel.shape[0]
    columns = product(hankel, start_basis)
    left = orthonormal(columns, total)
    across = product(hankel.T, left)
    lower_w = jnp.linalg.cholesky(product(across.T, across))
    right = right_solve(across, lower_w)
    columns = product(hankel, right)
    image = product(shifted, right)
    basis = orthonormal(columns, total)
    operator = product(basis.T, image) * (1.0 / math.sqrt(total))
    return (basis, operator)
```

```python
import functools
import math

import jax
import jax.numpy as jnp
from jax import lax
from jax.experimental import pallas as pl
from jax.experimental.pallas import tpu as pltpu
from jax.sharding import PartitionSpec as P

MESH = pl.DeviceIdType.MESH
NT = (((1,), (1,)), ((), ()))
VMEM_LIMIT = 48 * 1024 * 1024


def product(left, right, dims=(((1,), (0,)), ((), ()))):
    return lax.dot_general(
        left, right, dims, precision=lax.Precision.HIGHEST, preferred_element_type=jnp.float32
    )


def wait_bytes(ref, sem):
    pltpu.make_async_copy(ref, ref, sem).wait()


def exchange_kernel(
    n_rows, n_cols, hankel, shifted, start, y_out, c_out, z_out,
    h_slab, s_slab, parts, landed, sums, local_sem, slab_send, slab_recv, part_send, part_recv, sum_send, sum_recv,
):
    n = n_rows * n_cols
    row, col = lax.axis_index("rows"), lax.axis_index("cols")
    me = col * n_rows + row
    sub = h_slab.shape[2]
    prefixes = y_out.shape[0]
    share = prefixes // n

    def others(body):
        def step(k, carry):
            other = lax.rem(me + k, n)
            body(k, {"rows": lax.rem(other, n_rows), "cols": other // n_rows})
            return carry

        lax.fori_loop(1, n, step, 0)

    def own_copy(source, slab, which):
        columns = pl.ds(pl.multiple_of(row * sub, sub), sub)
        return pltpu.make_async_copy(source.at[:, columns], slab.at[row], local_sem.at[which])

    def send_slabs(source, slab, which):
        def step(k, carry):
            there = lax.rem(row + k, n_rows)
            columns = pl.ds(pl.multiple_of(there * sub, sub), sub)
            pltpu.make_async_remote_copy(
                src_ref=source.at[:, columns],
                dst_ref=slab.at[row],
                send_sem=slab_send.at[which],
                recv_sem=slab_recv.at[which],
                device_id={"rows": there, "cols": col},
                device_id_type=MESH,
            ).start()
            return carry

        lax.fori_loop(1, n_rows, step, 0)

    def whole(slab):
        return slab[...].reshape(prefixes, sub)

    def scatter(value, which):
        if share % 8 == 0:
            parts[which] = value.reshape(n, share, value.shape[1])
        else:
            for i in range(n):
                parts[which, i] = value[i * share : (i + 1) * share]
        landed[which, 0] = parts[which, me]

        def body(k, device):
            other = lax.rem(me + k, n)
            pltpu.make_async_remote_copy(
                src_ref=parts.at[which, other],
                dst_ref=landed.at[which, k],
                send_sem=part_send.at[which],
                recv_sem=part_recv.at[which],
                device_id=device,
                device_id_type=MESH,
            ).start()

        others(body)

    def gather(which):
        wait_bytes(landed.at[which, pl.ds(1, n - 1)], part_recv.at[which])
        sums[which, me] = jnp.sum(landed[which], axis=0)

        def body(k, device):
            pltpu.make_async_remote_copy(
                src_ref=sums.at[which, me],
                dst_ref=sums.at[which, me],
                send_sem=sum_send.at[which],
                recv_sem=sum_recv.at[which],
                device_id=device,
                device_id_type=MESH,
            ).start()

        others(body)

    def gathered(which, out):
        wait_bytes(sums.at[which, pl.ds(0, n - 1)], sum_recv.at[which])
        if share % 8 == 0:
            out[...] = sums[which].reshape(out.shape)
        else:
            for i in range(n):
                out[i * share : (i + 1) * share, :] = sums[which, i]

    own_copy(hankel, h_slab, 0).start()
    own_copy(shifted, s_slab, 1).start()
    barrier = pltpu.get_barrier_semaphore()
    others(lambda k, device: pl.semaphore_signal(barrier, inc=1, device_id=device, device_id_type=MESH))
    pl.semaphore_wait(barrier, n - 1)

    send_slabs(hankel, h_slab, 0)
    own_copy(hankel, h_slab, 0).wait()
    wait_bytes(h_slab.at[pl.ds(0, n_rows - 1)], slab_recv.at[0])
    scatter(product(whole(h_slab), start[...]), 0)
    send_slabs(shifted, s_slab, 1)
    block = whole(h_slab)
    gram = product(block, block, NT)
    gather(0)
    gathered(0, y_out)
    scatter(product(gram, y_out[...]), 1)
    gather(1)
    gathered(1, c_out)

    own_copy(shifted, s_slab, 1).wait()
    wait_bytes(s_slab.at[pl.ds(0, n_rows - 1)], slab_recv.at[1])
    cross = product(whole(s_slab), whole(h_slab), NT)
    scatter(product(cross, y_out[...]), 2)
    gather(2)
    gathered(2, z_out)

    for which in range(2):
        wait_bytes(h_slab.at[pl.ds(0, n_rows - 1)], slab_send.at[which])
    for which in range(3):
        wait_bytes(parts.at[which, pl.ds(0, n - 1)], part_send.at[which])
        wait_bytes(sums.at[which, pl.ds(0, n - 1)], sum_send.at[which])


def exchange(hankel, shifted, start):
    n_rows, n_cols = lax.axis_size("rows"), lax.axis_size("cols")
    n = n_rows * n_cols
    rows_dev, cols_dev = hankel.shape
    prefixes, sub, rank = rows_dev * n_rows, cols_dev // n_rows, start.shape[1]
    result = jax.ShapeDtypeStruct((prefixes, rank), jnp.float32)
    return pl.pallas_call(
        functools.partial(exchange_kernel, n_rows, n_cols),
        out_shape=[result] * 3,
        in_specs=[pl.BlockSpec(memory_space=pl.ANY)] * 2 + [pl.BlockSpec(memory_space=pltpu.VMEM)],
        out_specs=[pl.BlockSpec(memory_space=pltpu.VMEM)] * 3,
        scratch_shapes=[
            pltpu.VMEM((n_rows, rows_dev, sub), jnp.float32),
            pltpu.VMEM((n_rows, rows_dev, sub), jnp.float32),
            pltpu.VMEM((3, n, prefixes // n, rank), jnp.float32),
            pltpu.VMEM((3, n, prefixes // n, rank), jnp.float32),
            pltpu.VMEM((3, n, prefixes // n, rank), jnp.float32),
            pltpu.SemaphoreType.DMA((2,)),
            pltpu.SemaphoreType.DMA((2,)),
            pltpu.SemaphoreType.DMA((2,)),
            pltpu.SemaphoreType.DMA((3,)),
            pltpu.SemaphoreType.DMA((3,)),
            pltpu.SemaphoreType.DMA((3,)),
            pltpu.SemaphoreType.DMA((3,)),
        ],
        compiler_params=pltpu.CompilerParams(
            collective_id=0, has_side_effects=True, vmem_limit_bytes=VMEM_LIMIT
        ),
    )(hankel, shifted, start)


def invert_factors(grams, outs):
    size = grams[0].shape[0]
    lane = lax.broadcasted_iota(jnp.int32, (8, size), 1)
    sublane = lax.broadcasted_iota(jnp.int32, (8, size), 0)
    line = lax.broadcasted_iota(jnp.int32, (1, size), 1)
    tiles = [[gram[i : i + 8] for i in range(0, size, 8)] for gram in grams]
    for j in range(size):
        first, r = divmod(j, 8)
        for held, out in zip(tiles, outs):
            pivot = held[first][r : r + 1]
            diagonal = pivot[:, j : j + 1]
            inverse = 1.0 / diagonal
            scaled = jnp.broadcast_to(jnp.where(line == j, inverse, pivot * inverse), (8, size))
            out[j : j + 1, :] = jnp.where(line < j, pivot, jnp.where(line == j, 1.0, 0.0)) * lax.rsqrt(diagonal)
            for i in range(first, size // 8):
                column = held[i][:, j : j + 1]
                kept = jnp.where(lane == j, 0.0, held[i]) - column * scaled
                held[i] = jnp.where(sublane > r, kept, held[i]) if i == first else kept


def factor_kernel(y_ref, c_ref, z_ref, basis_ref, operator_ref, right_inv, left_inv):
    prefixes = c_ref.shape[0]
    rows_dev = basis_ref.shape[0]
    c = c_ref[...]
    c_t = c.T
    right_gram = product(y_ref[...].T, c)
    left_gram = product(c_t, c) * (1.0 / prefixes)
    crossed = product(c_t, z_ref[...]) * (1.0 / math.sqrt(prefixes))
    invert_factors((right_gram, left_gram), (right_inv, left_inv))
    mine = pl.ds(pl.multiple_of(lax.axis_index("rows") * rows_dev, rows_dev), rows_dev)
    basis_ref[...] = product(c_ref[mine, :], left_inv[...], NT)
    operator_ref[...] = product(product(left_inv[...], crossed), right_inv[...], NT)


def on_device(hankel, shifted, start_basis):
    y, c, z = exchange(hankel, shifted, start_basis)
    rank = start_basis.shape[1]
    return pl.pallas_call(
        factor_kernel,
        out_shape=[
            jax.ShapeDtypeStruct((hankel.shape[0], rank), jnp.float32),
            jax.ShapeDtypeStruct((rank, rank), jnp.float32),
        ],
        in_specs=[pl.BlockSpec(memory_space=pltpu.VMEM)] * 3,
        out_specs=[pl.BlockSpec(memory_space=pltpu.VMEM)] * 2,
        scratch_shapes=[pltpu.VMEM((rank, rank), jnp.float32)] * 2,
        compiler_params=pltpu.CompilerParams(vmem_limit_bytes=VMEM_LIMIT),
    )(y, c, z)


def solution(mesh):
    return jax.shard_map(
        on_device,
        mesh=mesh,
        in_specs=(P("rows", "cols"), P("rows", "cols"), P(("cols", "rows"), None)),
        out_specs=(P("rows", None), P()),
        check_vma=False,
    )
```

```python
import functools
import math

import jax
import jax.numpy as jnp
from jax import lax
from jax.experimental import pallas as pl
from jax.experimental.pallas import tpu as pltpu
from jax.sharding import PartitionSpec as P

MESH = pl.DeviceIdType.MESH
NT = (((1,), (1,)), ((), ()))
VMEM_LIMIT = 48 * 1024 * 1024


def product(left, right, dims=(((1,), (0,)), ((), ()))):
    return lax.dot_general(
        left, right, dims, precision=lax.Precision.HIGHEST, preferred_element_type=jnp.float32
    )


def wait_bytes(ref, sem):
    pltpu.make_async_copy(ref, ref, sem).wait()


def eliminate(begin, end, grams):
    size = grams[0].shape[0]
    height = 8
    lane = lax.broadcasted_iota(jnp.int32, (size, size), 1)
    place = lax.broadcasted_iota(jnp.int32, (size, size), 0)
    line = lax.broadcasted_iota(jnp.int32, (1, size), 1)

    def block(b, held):
        held = list(held)
        pending = size - height * b
        for r in range(height):
            active = (place > r) & (place < pending)
            known = (line < r) | (line >= pending)
            for m, values in enumerate(held):
                pivot = values[r : r + 1]
                diagonal = pivot[:, r : r + 1]
                inverse = 1.0 / diagonal
                scaled = jnp.where(line == r, inverse, pivot * inverse)
                final = jnp.where(known, pivot, jnp.where(line == r, 1.0, 0.0)) * lax.rsqrt(diagonal)
                kept = jnp.where(lane == r, 0.0, values) - values[:, r : r + 1] * scaled
                held[m] = jnp.where(active, kept, jnp.where(place == r, final, values))
        return tuple(
            pltpu.roll(jnp.concatenate([values[height:], values[:height]], axis=0), size - height, 1)
            for values in held
        )

    return lax.fori_loop(begin, end, block, grams)


def spectral_kernel(
    n_rows, n_cols, near, hankel, shifted, start, basis_out, operator_out,
    h_slab, s_slab, begun, parts, landed, middle, sums, local_sem, slab_send, slab_recv,
    part_send, part_recv, mid_send, mid_recv, sum_send, sum_recv,
):
    row, col = lax.axis_index("rows"), lax.axis_index("cols")
    layer, place = row // near, lax.rem(row, near)
    n_layers, n_group = n_rows // near, near * n_cols
    me = col * near + place
    rows_dev, sub = h_slab.shape[1:]
    prefixes = rows_dev * n_rows
    share = prefixes // n_group
    pieces = rows_dev // 8

    def loop(count, body):
        def step(k, carry):
            body(k)
            return carry

        lax.fori_loop(1, count, step, 0)

    def in_group(k):
        other = lax.rem(me + k, n_group)
        return other, {"rows": layer * near + lax.rem(other, near), "cols": other // near}

    def in_rows(k):
        other = lax.rem(row + k, n_rows)
        return other, {"rows": other, "cols": col}

    def in_layers(k):
        other = lax.rem(layer + k, n_layers)
        return other, {"rows": other * near + place, "cols": col}

    def send(source, target, sent, received, device):
        pltpu.make_async_remote_copy(
            src_ref=source,
            dst_ref=target,
            send_sem=sent,
            recv_sem=received,
            device_id=device,
            device_id_type=MESH,
        ).start()

    def own_columns(index):
        return pl.ds(pl.multiple_of(index * sub, sub), sub)

    def own_copy(source, slab, which):
        return pltpu.make_async_copy(source.at[:, own_columns(row)], slab.at[row], local_sem.at[which])

    def send_slabs(source, slab, which, lines):
        def body(k):
            other, device = in_rows(k)
            send(
                source.at[lines, own_columns(other)],
                slab.at[row, lines],
                slab_send.at[which],
                slab_recv.at[which],
                device,
            )

        loop(n_rows, body)

    def send_piece(piece):
        send_slabs(shifted, s_slab, 1, pl.ds(8 * piece, 8))

    def whole(slab):
        return slab[...].reshape(prefixes, sub)

    def scatter(value, which):
        parts[which] = value.reshape(n_group, share, value.shape[1])
        landed[which, 0] = parts[which, me]

        def body(k):
            other, device = in_group(k)
            send(parts.at[which, other], landed.at[which, k], part_send.at[which], part_recv.at[which], device)

        loop(n_group, body)

    def across(which):
        wait_bytes(landed.at[which, pl.ds(1, n_group - 1)], part_recv.at[which])
        middle[which, layer] = jnp.sum(landed[which], axis=0)
        mine = middle.at[which, layer]
        loop(n_layers, lambda k: send(mine, mine, mid_send.at[which], mid_recv.at[which], in_layers(k)[1]))

    def spread(which):
        wait_bytes(middle.at[which, pl.ds(0, n_layers - 1)], mid_recv.at[which])
        sums[which, me] = jnp.sum(middle[which], axis=0)
        mine = sums.at[which, me]
        loop(n_group, lambda k: send(mine, mine, sum_send.at[which], sum_recv.at[which], in_group(k)[1]))

    def total(which):
        wait_bytes(sums.at[which, pl.ds(0, n_group - 1)], sum_recv.at[which])
        return sums[which].reshape(prefixes, sums.shape[3])

    own_copy(hankel, h_slab, 0).start()
    own_copy(shifted, s_slab, 1).start()
    begin_copy = pltpu.make_async_copy(start, begun, local_sem.at[2])
    begin_copy.start()
    barrier = pltpu.get_barrier_semaphore()

    def greet(device):
        pl.semaphore_signal(barrier, inc=1, device_id=device, device_id_type=MESH)

    loop(n_rows, lambda k: greet(in_rows(k)[1]))
    loop(n_group, lambda k: greet(in_group(k)[1]))
    pl.semaphore_wait(barrier, n_rows + n_group - 2)

    send_slabs(hankel, h_slab, 0, pl.ds(0, rows_dev))
    own_copy(hankel, h_slab, 0).wait()
    begin_copy.wait()
    wait_bytes(h_slab.at[pl.ds(0, n_rows - 1)], slab_recv.at[0])
    scatter(product(whole(h_slab), begun[...]), 0)
    send_piece(0)
    block = whole(h_slab)
    gram = product(block, block, NT)
    across(0)
    for piece in range(1, pieces - 1):
        send_piece(piece)
    spread(0)
    y = total(0)
    scatter(product(gram, y), 1)
    y_t = y.T
    back = product(y_t, whole(h_slab))
    across(1)
    send_piece(pieces - 1)
    spread(1)
    c = total(1)
    c_t = c.T

    grams = (product(y_t, c), product(c_t, c) * (1.0 / prefixes))
    blocks = grams[0].shape[0] // 8
    cuts = (blocks // 4, blocks // 2, 3 * blocks // 4)
    grams = eliminate(0, cuts[0], grams)
    own_copy(shifted, s_slab, 1).wait()
    wait_bytes(s_slab.at[pl.ds(0, n_rows - 1)], slab_recv.at[1])
    scatter(product(whole(s_slab), back, NT), 2)
    grams = eliminate(cuts[0], cuts[1], grams)
    across(2)
    grams = eliminate(cuts[1], cuts[2], grams)
    spread(2)
    right_inv, left_inv = eliminate(cuts[2], blocks, grams)
    mine = sums.at[1].reshape(prefixes, c.shape[1])
    basis_out[...] = product(
        mine[pl.ds(pl.multiple_of(row * rows_dev, rows_dev), rows_dev), :], left_inv, NT
    )
    crossed = product(c_t, total(2)) * (1.0 / math.sqrt(prefixes))
    operator_out[...] = product(product(left_inv, crossed), right_inv, NT)

    for which in range(2):
        wait_bytes(h_slab.at[pl.ds(0, n_rows - 1)], slab_send.at[which])
    for which in range(3):
        wait_bytes(parts.at[which, pl.ds(0, n_group - 1)], part_send.at[which])
        wait_bytes(middle.at[which, pl.ds(0, n_layers - 1)], mid_send.at[which])
        wait_bytes(sums.at[which, pl.ds(0, n_group - 1)], sum_send.at[which])


def on_device(hankel, shifted, start_basis):
    n_rows, n_cols = lax.axis_size("rows"), lax.axis_size("cols")
    near = 2
    n_group = near * n_cols
    rows_dev, cols_dev = hankel.shape
    sub, rank = cols_dev // n_rows, start_basis.shape[1]
    share = rows_dev * n_rows // n_group
    slab = pltpu.VMEM((n_rows, rows_dev, sub), jnp.float32)
    grouped = pltpu.VMEM((3, n_group, share, rank), jnp.float32)
    return pl.pallas_call(
        functools.partial(spectral_kernel, n_rows, n_cols, near),
        out_shape=[
            jax.ShapeDtypeStruct((rows_dev, rank), jnp.float32),
            jax.ShapeDtypeStruct((rank, rank), jnp.float32),
        ],
        in_specs=[pl.BlockSpec(memory_space=pltpu.HBM)] * 3,
        out_specs=[pl.BlockSpec(memory_space=pltpu.VMEM)] * 2,
        scratch_shapes=[
            slab,
            slab,
            pltpu.VMEM((sub, rank), jnp.float32),
            grouped,
            grouped,
            pltpu.VMEM((3, n_rows // near, share, rank), jnp.float32),
            grouped,
            pltpu.SemaphoreType.DMA((3,)),
            pltpu.SemaphoreType.DMA((2,)),
            pltpu.SemaphoreType.DMA((2,)),
        ]
        + [pltpu.SemaphoreType.DMA((3,))] * 6,
        compiler_params=pltpu.CompilerParams(
            collective_id=0, has_side_effects=True, vmem_limit_bytes=VMEM_LIMIT
        ),
    )(hankel, shifted, start_basis)


def solution(mesh):
    return jax.shard_map(
        on_device,
        mesh=mesh,
        in_specs=(P("rows", "cols"), P("rows", "cols"), P(("cols", "rows"), None)),
        out_specs=(P("rows", None), P()),
        check_vma=False,
    )
```

```python
import functools
import math

import jax
import jax.numpy as jnp
from jax import lax
from jax.experimental import pallas as pl
from jax.experimental.pallas import tpu as pltpu
from jax.sharding import PartitionSpec as P

MESH = pl.DeviceIdType.MESH
NT = (((1,), (1,)), ((), ()))
VMEM_LIMIT = 64 * 1024 * 1024 - 256 * 1024


def product(left, right, dims=(((1,), (0,)), ((), ()))):
    return lax.dot_general(
        left, right, dims, precision=lax.Precision.HIGHEST, preferred_element_type=jnp.float32
    )


def wait_bytes(ref, sem):
    pltpu.make_async_copy(ref, ref, sem).wait()


def eliminate(begin, end, grams):
    size = grams[0].shape[0]
    height = 8
    limit = size - height * begin
    lane = lax.broadcasted_iota(jnp.int32, (limit, size), 1)
    place = lax.broadcasted_iota(jnp.int32, (limit, size), 0)
    line = lax.broadcasted_iota(jnp.int32, (1, size), 1)

    def block(b, held):
        live = [values[:limit] for values in held]
        pending = size - height * b
        for r in range(0, height, 2):
            active = (place > r + 1) & (place < pending)
            cleared = (lane == r) | (lane == r + 1)
            known = (line < r) | (line >= pending)
            for m, values in enumerate(live):
                p, q = values[r : r + 1], values[r + 1 : r + 2]
                d_pp, d_pq, d_qq = p[:, r : r + 1], p[:, r + 1 : r + 2], q[:, r + 1 : r + 2]
                det = d_pp * d_qq - d_pq * d_pq
                inverse = 1.0 / det
                i_pp, i_pq, i_qq = d_qq * inverse, d_pq * inverse, d_pp * inverse
                first = jnp.where(line == r, i_pp, jnp.where(line == r + 1, -i_pq, p * i_pp - q * i_pq))
                second = jnp.where(line == r, -i_pq, jnp.where(line == r + 1, i_qq, q * i_qq - p * i_pq))
                kept = (
                    jnp.where(cleared, 0.0, values)
                    - values[:, r : r + 1] * first
                    - values[:, r + 1 : r + 2] * second
                )
                p_known = jnp.where(known, p, jnp.where(line == r, 1.0, 0.0))
                q_known = jnp.where(known, q, jnp.where(line == r + 1, 1.0, 0.0))
                upper = p_known * lax.rsqrt(d_pp)
                under = (q_known - p_known * (d_pq / d_pp)) * lax.rsqrt(det / d_pp)
                done = jnp.where(place == r, upper, jnp.where(place == r + 1, under, values))
                live[m] = jnp.where(active, kept, done)
        return tuple(
            pltpu.roll(
                jnp.concatenate([x for x in (new[height:], values[limit:], new[:height]) if x.size], axis=0),
                size - height,
                1,
            )
            for new, values in zip(live, held)
        )

    return lax.fori_loop(begin, end, block, grams)


def unit_scaled(gram):
    corner = gram[:1, :1]
    return gram * (1.0 / corner), lax.rsqrt(corner)


def spectral_kernel(
    n_rows, n_cols, near, hankel, shifted, start, basis_out, operator_out,
    h_slab, s_slab, begun, parts, landed, middle, sums, local_sem, slab_send, slab_recv,
    part_send, part_recv, mid_send, mid_recv, sum_send, sum_recv,
):
    row, col = lax.axis_index("rows"), lax.axis_index("cols")
    layer, place = row // near, lax.rem(row, near)
    n_layers, n_group = n_rows // near, near * n_cols
    me = col * near + place
    rows_dev, sub = h_slab.shape[1:]
    prefixes = rows_dev * n_rows
    share = prefixes // n_group
    pieces = rows_dev // 8

    def loop(count, body):
        def step(k, carry):
            body(k)
            return carry

        lax.fori_loop(1, count, step, 0)

    def in_group(k):
        other = lax.rem(me + k, n_group)
        return other, {"rows": layer * near + lax.rem(other, near), "cols": other // near}

    def in_rows(k):
        other = lax.rem(row + k, n_rows)
        return other, {"rows": other, "cols": col}

    def in_layers(k):
        other = lax.rem(layer + k, n_layers)
        return other, {"rows": other * near + place, "cols": col}

    def send(source, target, sent, received, device):
        pltpu.make_async_remote_copy(
            src_ref=source,
            dst_ref=target,
            send_sem=sent,
            recv_sem=received,
            device_id=device,
            device_id_type=MESH,
        ).start()

    def own_columns(index):
        return pl.ds(pl.multiple_of(index * sub, sub), sub)

    def own_copy(source, slab, which):
        return pltpu.make_async_copy(source.at[:, own_columns(row)], slab.at[row], local_sem.at[which])

    def send_slabs(source, slab, which, lines):
        def body(k):
            other, device = in_rows(k)
            send(
                source.at[lines, own_columns(other)],
                slab.at[row, lines],
                slab_send.at[which],
                slab_recv.at[which],
                device,
            )

        loop(n_rows, body)

    def send_piece(piece):
        send_slabs(shifted, s_slab, 1, pl.ds(8 * piece, 8))

    def whole(slab):
        return slab[...].reshape(prefixes, sub)

    def scatter(value, which):
        parts[which] = value.reshape(n_group, share, value.shape[1])
        landed[which, 0] = parts[which, me]

        def body(k):
            other, device = in_group(k)
            send(parts.at[which, other], landed.at[which, k], part_send.at[which], part_recv.at[which], device)

        loop(n_group, body)

    def across(which):
        wait_bytes(landed.at[which, pl.ds(1, n_group - 1)], part_recv.at[which])
        middle[which, layer] = jnp.sum(landed[which], axis=0)
        mine = middle.at[which, layer]
        loop(n_layers, lambda k: send(mine, mine, mid_send.at[which], mid_recv.at[which], in_layers(k)[1]))

    def spread(which):
        wait_bytes(middle.at[which, pl.ds(0, n_layers - 1)], mid_recv.at[which])
        sums[which, me] = jnp.sum(middle[which], axis=0)
        mine = sums.at[which, me]
        loop(n_group, lambda k: send(mine, mine, sum_send.at[which], sum_recv.at[which], in_group(k)[1]))

    def total(which):
        wait_bytes(sums.at[which, pl.ds(0, n_group - 1)], sum_recv.at[which])
        return sums[which].reshape(prefixes, sums.shape[3])

    own_copy(hankel, h_slab, 0).start()
    own_copy(shifted, s_slab, 1).start()
    begin_copy = pltpu.make_async_copy(start, begun, local_sem.at[2])
    begin_copy.start()
    barrier = pltpu.get_barrier_semaphore()

    def greet(device):
        pl.semaphore_signal(barrier, inc=1, device_id=device, device_id_type=MESH)

    loop(n_rows, lambda k: greet(in_rows(k)[1]))
    loop(n_group, lambda k: greet(in_group(k)[1]))
    pl.semaphore_wait(barrier, n_rows + n_group - 2)

    send_slabs(hankel, h_slab, 0, pl.ds(0, rows_dev))
    own_copy(hankel, h_slab, 0).wait()
    begin_copy.wait()
    wait_bytes(h_slab.at[pl.ds(0, n_rows - 1)], slab_recv.at[0])
    scatter(product(whole(h_slab), begun[...]), 0)
    block = whole(h_slab)
    gram = product(block, block, NT)
    across(0)
    send_piece(0)
    spread(0)
    y = total(0)
    scatter(product(gram, y), 1)
    y_t = y.T
    back = product(y_t, whole(h_slab))
    across(1)
    send_piece(1)
    spread(1)
    for piece in range(2, pieces):
        send_piece(piece)
    c = total(1)
    c_t = c.T

    right_gram, right_scale = unit_scaled(product(y_t, c))
    left_gram, left_scale = unit_scaled(product(c_t, c) * (1.0 / prefixes))
    grams = (right_gram, left_gram)
    blocks = right_gram.shape[0] // 8
    cuts = (3 * blocks // 8, 5 * blocks // 8, 13 * blocks // 16)
    grams = eliminate(0, cuts[0], grams)
    own_copy(shifted, s_slab, 1).wait()
    wait_bytes(s_slab.at[pl.ds(0, n_rows - 1)], slab_recv.at[1])
    scatter(product(whole(s_slab), back, NT), 2)
    grams = eliminate(cuts[0], cuts[1], grams)
    across(2)
    grams = eliminate(cuts[1], cuts[2], grams)
    spread(2)
    right_inv, left_inv = eliminate(cuts[2], blocks, grams)
    right_inv, left_inv = right_inv * right_scale, left_inv * left_scale
    mine = sums.at[1].reshape(prefixes, c.shape[1])
    basis_out[...] = product(
        mine[pl.ds(pl.multiple_of(row * rows_dev, rows_dev), rows_dev), :], left_inv, NT
    )
    crossed = product(c_t, total(2)) * (1.0 / math.sqrt(prefixes))
    operator_out[...] = product(product(left_inv, crossed), right_inv, NT)

    for which in range(2):
        wait_bytes(h_slab.at[pl.ds(0, n_rows - 1)], slab_send.at[which])
    for which in range(3):
        wait_bytes(parts.at[which, pl.ds(0, n_group - 1)], part_send.at[which])
        wait_bytes(middle.at[which, pl.ds(0, n_layers - 1)], mid_send.at[which])
        wait_bytes(sums.at[which, pl.ds(0, n_group - 1)], sum_send.at[which])


def on_device(hankel, shifted, start_basis):
    n_rows, n_cols = lax.axis_size("rows"), lax.axis_size("cols")
    near = 2
    n_group = near * n_cols
    rows_dev, cols_dev = hankel.shape
    sub, rank = cols_dev // n_rows, start_basis.shape[1]
    share = rows_dev * n_rows // n_group
    slab = pltpu.VMEM((n_rows, rows_dev, sub), jnp.float32)
    grouped = pltpu.VMEM((3, n_group, share, rank), jnp.float32)
    return pl.pallas_call(
        functools.partial(spectral_kernel, n_rows, n_cols, near),
        out_shape=[
            jax.ShapeDtypeStruct((rows_dev, rank), jnp.float32),
            jax.ShapeDtypeStruct((rank, rank), jnp.float32),
        ],
        in_specs=[pl.BlockSpec(memory_space=pltpu.HBM)] * 3,
        out_specs=[pl.BlockSpec(memory_space=pltpu.VMEM)] * 2,
        scratch_shapes=[
            slab,
            slab,
            pltpu.VMEM((sub, rank), jnp.float32),
            grouped,
            grouped,
            pltpu.VMEM((3, n_rows // near, share, rank), jnp.float32),
            grouped,
            pltpu.SemaphoreType.DMA((3,)),
            pltpu.SemaphoreType.DMA((2,)),
            pltpu.SemaphoreType.DMA((2,)),
        ]
        + [pltpu.SemaphoreType.DMA((3,))] * 6,
        compiler_params=pltpu.CompilerParams(
            collective_id=0, has_side_effects=True, vmem_limit_bytes=VMEM_LIMIT
        ),
    )(hankel, shifted, start_basis)


def solution(mesh):
    return jax.shard_map(
        on_device,
        mesh=mesh,
        in_specs=(P("rows", "cols"), P("rows", "cols"), P(("cols", "rows"), None)),
        out_specs=(P("rows", None), P()),
        check_vma=False,
    )
```

```python
import functools
import math

import jax
import jax.numpy as jnp
from jax import lax
from jax.experimental import pallas as pl
from jax.experimental.pallas import tpu as pltpu
from jax.sharding import PartitionSpec as P

MESH = pl.DeviceIdType.MESH
NT = (((1,), (1,)), ((), ()))
VMEM_LIMIT = 64 * 1024 * 1024 - 480 * 1024


def product(left, right, dims=(((1,), (0,)), ((), ()))):
    return lax.dot_general(
        left, right, dims, precision=lax.Precision.HIGHEST, preferred_element_type=jnp.float32
    )


def wait_bytes(ref, sem):
    pltpu.make_async_copy(ref, ref, sem).wait()


def eliminate(begin, end, grams):
    size = grams[0].shape[0]
    height = 8
    limit = size - height * begin
    lane = lax.broadcasted_iota(jnp.int32, (limit, size), 1)
    place = lax.broadcasted_iota(jnp.int32, (limit, size), 0)
    line = lax.broadcasted_iota(jnp.int32, (1, size), 1)

    def block(b, held):
        live = [values[:limit] for values in held]
        pending = size - height * b
        for r in range(0, height, 2):
            active = (place > r + 1) & (place < pending)
            cleared = (lane == r) | (lane == r + 1)
            known = (line < r) | (line >= pending)
            for m, values in enumerate(live):
                p, q = values[r : r + 1], values[r + 1 : r + 2]
                d_pp, d_pq, d_qq = p[:, r : r + 1], p[:, r + 1 : r + 2], q[:, r + 1 : r + 2]
                det = d_pp * d_qq - d_pq * d_pq
                inverse = 1.0 / det
                i_pp, i_pq, i_qq = d_qq * inverse, d_pq * inverse, d_pp * inverse
                first = jnp.where(line == r, i_pp, jnp.where(line == r + 1, -i_pq, p * i_pp - q * i_pq))
                second = jnp.where(line == r, -i_pq, jnp.where(line == r + 1, i_qq, q * i_qq - p * i_pq))
                kept = (
                    jnp.where(cleared, 0.0, values)
                    - values[:, r : r + 1] * first
                    - values[:, r + 1 : r + 2] * second
                )
                p_known = jnp.where(known, p, jnp.where(line == r, 1.0, 0.0))
                q_known = jnp.where(known, q, jnp.where(line == r + 1, 1.0, 0.0))
                upper = p_known * lax.rsqrt(d_pp)
                under = (q_known - p_known * (d_pq / d_pp)) * lax.rsqrt(det / d_pp)
                done = jnp.where(place == r, upper, jnp.where(place == r + 1, under, values))
                live[m] = jnp.where(active, kept, done)
        return tuple(
            pltpu.roll(
                jnp.concatenate([x for x in (new[height:], values[limit:], new[:height]) if x.size], axis=0),
                size - height,
                1,
            )
            for new, values in zip(live, held)
        )

    return lax.fori_loop(begin, end, block, grams)


def unit_scaled(gram):
    corner = gram[:1, :1]
    return gram * (1.0 / corner), lax.rsqrt(corner)


def spectral_kernel(
    n_rows, n_cols, near, hankel, shifted, start, basis_out, operator_out,
    h_slab, s_slab, begun, parts, landed, middle, sums, local_sem, slab_send, slab_recv,
    part_send, part_recv, mid_send, mid_recv, sum_send, sum_recv,
):
    row, col = lax.axis_index("rows"), lax.axis_index("cols")
    layer, place = row // near, lax.rem(row, near)
    n_layers, n_group = n_rows // near, near * n_cols
    me = col * near + place
    rows_dev, sub = h_slab.shape[1:]
    prefixes = rows_dev * n_rows
    share = prefixes // n_group
    pieces = rows_dev // 8

    def loop(count, body):
        def step(k, carry):
            body(k)
            return carry

        lax.fori_loop(1, count, step, 0)

    def in_group(k):
        other = lax.rem(me + k, n_group)
        return other, {"rows": layer * near + lax.rem(other, near), "cols": other // near}

    def in_rows(k):
        other = lax.rem(row + k, n_rows)
        return other, {"rows": other, "cols": col}

    def in_layers(k):
        other = lax.rem(layer + k, n_layers)
        return other, {"rows": other * near + place, "cols": col}

    def send(source, target, sent, received, device):
        pltpu.make_async_remote_copy(
            src_ref=source,
            dst_ref=target,
            send_sem=sent,
            recv_sem=received,
            device_id=device,
            device_id_type=MESH,
        ).start()

    def own_columns(index):
        return pl.ds(pl.multiple_of(index * sub, sub), sub)

    def own_copy(source, slab, which):
        return pltpu.make_async_copy(source.at[:, own_columns(row)], slab.at[row], local_sem.at[which])

    def send_slabs(source, slab, which, lines):
        def body(k):
            other, device = in_rows(k)
            send(
                source.at[lines, own_columns(other)],
                slab.at[row, lines],
                slab_send.at[which],
                slab_recv.at[which],
                device,
            )

        loop(n_rows, body)

    def send_piece(piece):
        send_slabs(shifted, s_slab, 1, pl.ds(8 * piece, 8))

    def whole(slab):
        return slab[...].reshape(prefixes, sub)

    def scatter(value, which):
        parts[which] = value.reshape(n_group, share, value.shape[1])
        landed[which, 0] = parts[which, me]

        def body(k):
            other, device = in_group(k)
            send(parts.at[which, other], landed.at[which, k], part_send.at[which], part_recv.at[which], device)

        loop(n_group, body)

    def across(which):
        wait_bytes(landed.at[which, pl.ds(1, n_group - 1)], part_recv.at[which])
        middle[which, layer] = jnp.sum(landed[which], axis=0)
        mine = middle.at[which, layer]
        loop(n_layers, lambda k: send(mine, mine, mid_send.at[which], mid_recv.at[which], in_layers(k)[1]))

    def spread(which):
        wait_bytes(middle.at[which, pl.ds(0, n_layers - 1)], mid_recv.at[which])
        sums[which, me] = jnp.sum(middle[which], axis=0)
        mine = sums.at[which, me]
        loop(n_group, lambda k: send(mine, mine, sum_send.at[which], sum_recv.at[which], in_group(k)[1]))

    def total(which):
        wait_bytes(sums.at[which, pl.ds(0, n_group - 1)], sum_recv.at[which])
        return sums[which].reshape(prefixes, sums.shape[3])

    own_copy(hankel, h_slab, 0).start()
    own_copy(shifted, s_slab, 1).start()
    begin_copy = pltpu.make_async_copy(start, begun, local_sem.at[2])
    begin_copy.start()
    barrier = pltpu.get_barrier_semaphore()

    def greet(device):
        pl.semaphore_signal(barrier, inc=1, device_id=device, device_id_type=MESH)

    loop(n_rows, lambda k: greet(in_rows(k)[1]))
    loop(n_group, lambda k: greet(in_group(k)[1]))
    pl.semaphore_wait(barrier, n_rows + n_group - 2)

    send_slabs(hankel, h_slab, 0, pl.ds(0, rows_dev))
    own_copy(hankel, h_slab, 0).wait()
    begin_copy.wait()
    wait_bytes(h_slab.at[pl.ds(0, n_rows - 1)], slab_recv.at[0])
    send_piece(0)
    scatter(product(whole(h_slab), begun[...]), 0)
    block = whole(h_slab)
    gram = product(block, block, NT)
    across(0)
    send_piece(1)
    spread(0)
    send_piece(2)
    y = total(0)
    scatter(product(gram, y), 1)
    y_t = y.T
    back = product(y_t, whole(h_slab))
    across(1)
    for piece in range(3, pieces):
        send_piece(piece)
    spread(1)
    c = total(1)
    c_t = c.T

    right_gram, right_scale = unit_scaled(product(y_t, c))
    left_gram, left_scale = unit_scaled(product(c_t, c) * (1.0 / prefixes))
    grams = (right_gram, left_gram)
    blocks = right_gram.shape[0] // 8
    cuts = (blocks // 8, 7 * blocks // 16, 11 * blocks // 16)
    grams = eliminate(0, cuts[0], grams)
    own_copy(shifted, s_slab, 1).wait()
    wait_bytes(s_slab.at[pl.ds(0, n_rows - 1)], slab_recv.at[1])
    scatter(product(whole(s_slab), back, NT), 2)
    grams = eliminate(cuts[0], cuts[1], grams)
    across(2)
    grams = eliminate(cuts[1], cuts[2], grams)
    spread(2)
    right_inv, left_inv = eliminate(cuts[2], blocks, grams)
    right_inv, left_inv = right_inv * right_scale, left_inv * left_scale
    mine = sums.at[1].reshape(prefixes, c.shape[1])
    basis_out[...] = product(
        mine[pl.ds(pl.multiple_of(row * rows_dev, rows_dev), rows_dev), :], left_inv, NT
    )
    crossed = product(c_t, total(2)) * (1.0 / math.sqrt(prefixes))
    operator_out[...] = product(product(left_inv, crossed), right_inv, NT)

    for which in range(2):
        wait_bytes(h_slab.at[pl.ds(0, n_rows - 1)], slab_send.at[which])
    for which in range(3):
        wait_bytes(parts.at[which, pl.ds(0, n_group - 1)], part_send.at[which])
        wait_bytes(middle.at[which, pl.ds(0, n_layers - 1)], mid_send.at[which])
        wait_bytes(sums.at[which, pl.ds(0, n_group - 1)], sum_send.at[which])


def on_device(hankel, shifted, start_basis):
    n_rows, n_cols = lax.axis_size("rows"), lax.axis_size("cols")
    near = 2
    n_group = near * n_cols
    rows_dev, cols_dev = hankel.shape
    sub, rank = cols_dev // n_rows, start_basis.shape[1]
    share = rows_dev * n_rows // n_group
    slab = pltpu.VMEM((n_rows, rows_dev, sub), jnp.float32)
    grouped = pltpu.VMEM((3, n_group, share, rank), jnp.float32)
    return pl.pallas_call(
        functools.partial(spectral_kernel, n_rows, n_cols, near),
        out_shape=[
            jax.ShapeDtypeStruct((rows_dev, rank), jnp.float32),
            jax.ShapeDtypeStruct((rank, rank), jnp.float32),
        ],
        in_specs=[pl.BlockSpec(memory_space=pltpu.HBM)] * 3,
        out_specs=[pl.BlockSpec(memory_space=pltpu.VMEM)] * 2,
        scratch_shapes=[
            slab,
            slab,
            pltpu.VMEM((sub, rank), jnp.float32),
            grouped,
            grouped,
            pltpu.VMEM((3, n_rows // near, share, rank), jnp.float32),
            grouped,
            pltpu.SemaphoreType.DMA((3,)),
            pltpu.SemaphoreType.DMA((2,)),
            pltpu.SemaphoreType.DMA((2,)),
        ]
        + [pltpu.SemaphoreType.DMA((3,))] * 6,
        compiler_params=pltpu.CompilerParams(
            collective_id=0, has_side_effects=True, vmem_limit_bytes=VMEM_LIMIT
        ),
    )(hankel, shifted, start_basis)


def solution(mesh):
    return jax.shard_map(
        on_device,
        mesh=mesh,
        in_specs=(P("rows", "cols"), P("rows", "cols"), P(("cols", "rows"), None)),
        out_specs=(P("rows", None), P()),
        check_vma=False,
    )
```

```python
import functools
import math

import jax
import jax.numpy as jnp
from jax import lax
from jax.experimental import pallas as pl
from jax.experimental.pallas import tpu as pltpu
from jax.sharding import PartitionSpec as P

MESH = pl.DeviceIdType.MESH
NT = (((1,), (1,)), ((), ()))
VMEM_LIMIT = 64 * 1024 * 1024 - 480 * 1024


def product(left, right, dims=(((1,), (0,)), ((), ()))):
    return lax.dot_general(
        left, right, dims, precision=lax.Precision.HIGHEST, preferred_element_type=jnp.float32
    )


def wait_bytes(ref, sem):
    pltpu.make_async_copy(ref, ref, sem).wait()


def eliminate(begin, end, grams):
    height, size = grams[0][0].shape
    tiles = len(grams[0])
    lane = lax.broadcasted_iota(jnp.int32, (height, size), 1)
    sublane = lax.broadcasted_iota(jnp.int32, (height, size), 0)
    line = lax.broadcasted_iota(jnp.int32, (1, size), 1)

    def block(b, held):
        held = [list(matrix) for matrix in held]
        known_from = size - height * b
        for r in range(height):
            here = lane == r
            known = (line < r) | (line >= known_from)
            for matrix in held:
                pivot = matrix[0][r : r + 1]
                diagonal = pivot[:, r : r + 1]
                inverse = 1.0 / diagonal
                scaled = jnp.broadcast_to(jnp.where(line == r, inverse, pivot * inverse), (height, size))
                final = jnp.where(known, pivot, jnp.where(line == r, 1.0, 0.0)) * lax.rsqrt(diagonal)
                for i in range(tiles - begin):
                    values = matrix[i]
                    kept = jnp.where(here, 0.0, values) - values[:, r : r + 1] * scaled
                    if i == 0:
                        kept = jnp.where(sublane > r, kept, jnp.where(sublane == r, final, values))
                    elif i > tiles - end:
                        kept = jnp.where(i < tiles - b, kept, values)
                    matrix[i] = kept
        return tuple(
            tuple(pltpu.roll(values, size - height, 1) for values in matrix[1:] + matrix[:1]) for matrix in held
        )

    return lax.fori_loop(begin, end, block, grams)


def to_tiles(gram):
    return tuple(gram[i : i + 8] for i in range(0, gram.shape[0], 8))


def from_tiles(tiles):
    return jnp.concatenate(tiles, axis=0)


def spectral_kernel(
    n_rows, n_cols, near, hankel, shifted, start, basis_out, operator_out,
    h_own, s_own, h_slab, s_slab, begun, parts, landed, middle, sums, local_sem, slab_send, slab_recv,
    part_send, part_recv, mid_send, mid_recv, sum_send, sum_recv,
):
    row, col = lax.axis_index("rows"), lax.axis_index("cols")
    layer, place = row // near, lax.rem(row, near)
    n_layers, n_group = n_rows // near, near * n_cols
    me = col * near + place
    rows_dev, sub = h_slab.shape[1:]
    prefixes = rows_dev * n_rows
    share = prefixes // n_group
    pieces = rows_dev // 8

    def loop(count, body):
        def step(k, carry):
            body(k)
            return carry

        lax.fori_loop(1, count, step, 0)

    def in_group(k):
        other = lax.rem(me + k, n_group)
        return other, {"rows": layer * near + lax.rem(other, near), "cols": other // near}

    def in_rows(k):
        other = lax.rem(row + k, n_rows)
        return other, {"rows": other, "cols": col}

    def in_layers(k):
        other = lax.rem(layer + k, n_layers)
        return other, {"rows": other * near + place, "cols": col}

    def send(source, target, sent, received, device):
        pltpu.make_async_remote_copy(
            src_ref=source,
            dst_ref=target,
            send_sem=sent,
            recv_sem=received,
            device_id=device,
            device_id_type=MESH,
        ).start()

    def own_columns(index):
        return pl.ds(pl.multiple_of(index * sub, sub), sub)

    def own_copy(source, slab, which):
        return pltpu.make_async_copy(source.at[:, own_columns(row)], slab.at[row], local_sem.at[which])

    hankel_in = pltpu.make_async_copy(hankel, h_own, local_sem.at[3])
    shifted_in = pltpu.make_async_copy(shifted, s_own, local_sem.at[4])

    def send_slabs(source, slab, which, lines):
        def body(k):
            other, device = in_rows(k)
            send(
                source.at[lines, own_columns(other)],
                slab.at[row, lines],
                slab_send.at[which],
                slab_recv.at[which],
                device,
            )

        loop(n_rows, body)

    def send_piece(piece):
        send_slabs(s_own, s_slab, 1, pl.ds(8 * piece, 8))

    def whole(slab):
        return slab[...].reshape(prefixes, sub)

    def scatter(value, which):
        parts[which] = value.reshape(n_group, share, value.shape[1])
        landed[which, 0] = parts[which, me]

        def body(k):
            other, device = in_group(k)
            send(parts.at[which, other], landed.at[which, k], part_send.at[which], part_recv.at[which], device)

        loop(n_group, body)

    def across(which):
        wait_bytes(landed.at[which, pl.ds(1, n_group - 1)], part_recv.at[which])
        middle[which, layer] = jnp.sum(landed[which], axis=0)
        mine = middle.at[which, layer]
        loop(n_layers, lambda k: send(mine, mine, mid_send.at[which], mid_recv.at[which], in_layers(k)[1]))

    def spread(which):
        wait_bytes(middle.at[which, pl.ds(0, n_layers - 1)], mid_recv.at[which])
        sums[which, me] = jnp.sum(middle[which], axis=0)
        mine = sums.at[which, me]
        loop(n_group, lambda k: send(mine, mine, sum_send.at[which], sum_recv.at[which], in_group(k)[1]))

    def total(which):
        wait_bytes(sums.at[which, pl.ds(0, n_group - 1)], sum_recv.at[which])
        return sums[which].reshape(prefixes, sums.shape[3])

    hankel_in.start()
    own_copy(hankel, h_slab, 0).start()
    shifted_in.start()
    own_copy(shifted, s_slab, 1).start()
    begin_copy = pltpu.make_async_copy(start, begun, local_sem.at[2])
    begin_copy.start()
    barrier = pltpu.get_barrier_semaphore()

    def greet(device):
        pl.semaphore_signal(barrier, inc=1, device_id=device, device_id_type=MESH)

    loop(n_rows, lambda k: greet(in_rows(k)[1]))
    loop(n_group, lambda k: greet(in_group(k)[1]))
    pl.semaphore_wait(barrier, n_rows + n_group - 2)

    hankel_in.wait()
    send_slabs(h_own, h_slab, 0, pl.ds(0, rows_dev))
    shifted_in.wait()
    own_copy(hankel, h_slab, 0).wait()
    begin_copy.wait()
    wait_bytes(h_slab.at[pl.ds(0, n_rows - 1)], slab_recv.at[0])
    send_piece(0)
    scatter(product(whole(h_slab), begun[...]), 0)
    block = whole(h_slab)
    gram = product(block, block, NT)
    across(0)
    send_piece(1)
    spread(0)
    send_piece(2)
    y = total(0)
    scatter(product(gram, y), 1)
    y_t = y.T
    back = product(y_t, whole(h_slab))
    across(1)
    for piece in range(3, pieces):
        send_piece(piece)
    spread(1)
    c = total(1)
    c_t = c.T

    grams = (to_tiles(product(y_t, c)), to_tiles(product(c_t, c) * (1.0 / prefixes)))
    blocks = len(grams[0])
    cuts = (blocks // 8, 7 * blocks // 16, 11 * blocks // 16)
    grams = eliminate(0, cuts[0], grams)
    own_copy(shifted, s_slab, 1).wait()
    wait_bytes(s_slab.at[pl.ds(0, n_rows - 1)], slab_recv.at[1])
    scatter(product(whole(s_slab), back, NT), 2)
    grams = eliminate(cuts[0], cuts[1], grams)
    across(2)
    grams = eliminate(cuts[1], cuts[2], grams)
    spread(2)
    right_inv, left_inv = eliminate(cuts[2], blocks, grams)
    right_inv, left_inv = from_tiles(right_inv), from_tiles(left_inv)
    mine = sums.at[1].reshape(prefixes, c.shape[1])
    basis_out[...] = product(
        mine[pl.ds(pl.multiple_of(row * rows_dev, rows_dev), rows_dev), :], left_inv, NT
    )
    crossed = product(c_t, total(2)) * (1.0 / math.sqrt(prefixes))
    operator_out[...] = product(product(left_inv, crossed), right_inv, NT)

    for which in range(2):
        wait_bytes(h_slab.at[pl.ds(0, n_rows - 1)], slab_send.at[which])
    for which in range(3):
        wait_bytes(parts.at[which, pl.ds(0, n_group - 1)], part_send.at[which])
        wait_bytes(middle.at[which, pl.ds(0, n_layers - 1)], mid_send.at[which])
        wait_bytes(sums.at[which, pl.ds(0, n_group - 1)], sum_send.at[which])


def on_device(hankel, shifted, start_basis):
    n_rows, n_cols = lax.axis_size("rows"), lax.axis_size("cols")
    near = 2
    n_group = near * n_cols
    rows_dev, cols_dev = hankel.shape
    sub, rank = cols_dev // n_rows, start_basis.shape[1]
    share = rows_dev * n_rows // n_group
    slab = pltpu.VMEM((n_rows, rows_dev, sub), jnp.float32)
    grouped = pltpu.VMEM((3, n_group, share, rank), jnp.float32)
    return pl.pallas_call(
        functools.partial(spectral_kernel, n_rows, n_cols, near),
        out_shape=[
            jax.ShapeDtypeStruct((rows_dev, rank), jnp.float32),
            jax.ShapeDtypeStruct((rank, rank), jnp.float32),
        ],
        in_specs=[pl.BlockSpec(memory_space=pltpu.HBM)] * 3,
        out_specs=[pl.BlockSpec(memory_space=pltpu.VMEM)] * 2,
        scratch_shapes=[
            pltpu.VMEM((rows_dev, cols_dev), jnp.float32),
            pltpu.VMEM((rows_dev, cols_dev), jnp.float32),
            slab,
            slab,
            pltpu.VMEM((sub, rank), jnp.float32),
            grouped,
            grouped,
            pltpu.VMEM((3, n_rows // near, share, rank), jnp.float32),
            grouped,
            pltpu.SemaphoreType.DMA((5,)),
            pltpu.SemaphoreType.DMA((2,)),
            pltpu.SemaphoreType.DMA((2,)),
        ]
        + [pltpu.SemaphoreType.DMA((3,))] * 6,
        compiler_params=pltpu.CompilerParams(
            collective_id=0, has_side_effects=True, vmem_limit_bytes=VMEM_LIMIT
        ),
    )(hankel, shifted, start_basis)


def solution(mesh):
    return jax.shard_map(
        on_device,
        mesh=mesh,
        in_specs=(P("rows", "cols"), P("rows", "cols"), P(("cols", "rows"), None)),
        out_specs=(P("rows", None), P()),
        check_vma=False,
    )
```

```python
import functools
import math

import jax
import jax.numpy as jnp
from jax import lax
from jax.experimental import pallas as pl
from jax.experimental.pallas import tpu as pltpu
from jax.sharding import PartitionSpec as P

MESH = pl.DeviceIdType.MESH
NT = (((1,), (1,)), ((), ()))
VMEM_LIMIT = 64 * 1024 * 1024 - 480 * 1024


def product(left, right, dims=(((1,), (0,)), ((), ()))):
    return lax.dot_general(
        left, right, dims, precision=lax.Precision.HIGHEST, preferred_element_type=jnp.float32
    )


def split(values):
    high = values.astype(jnp.bfloat16)
    return high, (values - high.astype(jnp.float32)).astype(jnp.bfloat16)


def split_product(left, right, dims=(((1,), (0,)), ((), ()))):
    def term(a, b):
        return lax.dot_general(a, b, dims, preferred_element_type=jnp.float32)

    return term(left[0], right[0]) + (term(left[0], right[1]) + term(left[1], right[0]))


def wait_bytes(ref, sem):
    pltpu.make_async_copy(ref, ref, sem).wait()


def eliminate(begin, end, grams):
    height, size = grams[0][0].shape
    tiles = len(grams[0])
    lane = lax.broadcasted_iota(jnp.int32, (height, size), 1)
    sublane = lax.broadcasted_iota(jnp.int32, (height, size), 0)
    line = lax.broadcasted_iota(jnp.int32, (1, size), 1)

    def block(b, held):
        held = [list(matrix) for matrix in held]
        known_from = size - height * b
        for r in range(height):
            here = lane == r
            known = (line < r) | (line >= known_from)
            for matrix in held:
                pivot = matrix[0][r : r + 1]
                diagonal = pivot[:, r : r + 1]
                inverse = 1.0 / diagonal
                scaled = jnp.broadcast_to(jnp.where(line == r, inverse, pivot * inverse), (height, size))
                final = jnp.where(known, pivot, jnp.where(line == r, 1.0, 0.0)) * lax.rsqrt(diagonal)
                for i in range(tiles - begin):
                    values = matrix[i]
                    kept = jnp.where(here, 0.0, values) - values[:, r : r + 1] * scaled
                    if i == 0:
                        kept = jnp.where(sublane > r, kept, jnp.where(sublane == r, final, values))
                    elif i > tiles - end:
                        kept = jnp.where(i < tiles - b, kept, values)
                    matrix[i] = kept
        return tuple(
            tuple(pltpu.roll(values, size - height, 1) for values in matrix[1:] + matrix[:1]) for matrix in held
        )

    return lax.fori_loop(begin, end, block, grams)


def to_tiles(gram):
    return tuple(gram[i : i + 8] for i in range(0, gram.shape[0], 8))


def from_tiles(tiles):
    return jnp.concatenate(tiles, axis=0)


def spectral_kernel(
    n_rows, n_cols, near, hankel, shifted, start, basis_out, operator_out,
    h_own, s_own, h_slab, s_slab, begun, parts, landed, middle, sums, local_sem, slab_send, slab_recv,
    part_send, part_recv, mid_send, mid_recv, sum_send, sum_recv,
):
    row, col = lax.axis_index("rows"), lax.axis_index("cols")
    layer, place = row // near, lax.rem(row, near)
    n_layers, n_group = n_rows // near, near * n_cols
    me = col * near + place
    rows_dev, sub = h_slab.shape[1:]
    prefixes = rows_dev * n_rows
    share = prefixes // n_group
    pieces = rows_dev // 8

    def loop(count, body):
        def step(k, carry):
            body(k)
            return carry

        lax.fori_loop(1, count, step, 0)

    def in_group(k):
        other = lax.rem(me + k, n_group)
        return other, {"rows": layer * near + lax.rem(other, near), "cols": other // near}

    def in_rows(k):
        other = lax.rem(row + k, n_rows)
        return other, {"rows": other, "cols": col}

    def in_layers(k):
        other = lax.rem(layer + k, n_layers)
        return other, {"rows": other * near + place, "cols": col}

    def send(source, target, sent, received, device):
        pltpu.make_async_remote_copy(
            src_ref=source,
            dst_ref=target,
            send_sem=sent,
            recv_sem=received,
            device_id=device,
            device_id_type=MESH,
        ).start()

    def own_columns(index):
        return pl.ds(pl.multiple_of(index * sub, sub), sub)

    def own_copy(source, slab, which):
        return pltpu.make_async_copy(source.at[:, own_columns(row)], slab.at[row], local_sem.at[which])

    hankel_in = pltpu.make_async_copy(hankel, h_own, local_sem.at[3])
    shifted_in = pltpu.make_async_copy(shifted, s_own, local_sem.at[4])

    def send_slabs(source, slab, which, lines):
        def body(k):
            other, device = in_rows(k)
            send(
                source.at[lines, own_columns(other)],
                slab.at[row, lines],
                slab_send.at[which],
                slab_recv.at[which],
                device,
            )

        loop(n_rows, body)

    def send_piece(piece):
        send_slabs(s_own, s_slab, 1, pl.ds(8 * piece, 8))

    def whole(slab):
        return slab[...].reshape(prefixes, sub)

    def scatter(value, which):
        parts[which] = value.reshape(n_group, share, value.shape[1])
        landed[which, 0] = parts[which, me]

        def body(k):
            other, device = in_group(k)
            send(parts.at[which, other], landed.at[which, k], part_send.at[which], part_recv.at[which], device)

        loop(n_group, body)

    def across(which):
        wait_bytes(landed.at[which, pl.ds(1, n_group - 1)], part_recv.at[which])
        middle[which, layer] = jnp.sum(landed[which], axis=0)
        mine = middle.at[which, layer]
        loop(n_layers, lambda k: send(mine, mine, mid_send.at[which], mid_recv.at[which], in_layers(k)[1]))

    def spread(which):
        wait_bytes(middle.at[which, pl.ds(0, n_layers - 1)], mid_recv.at[which])
        sums[which, me] = jnp.sum(middle[which], axis=0)
        mine = sums.at[which, me]
        loop(n_group, lambda k: send(mine, mine, sum_send.at[which], sum_recv.at[which], in_group(k)[1]))

    def total(which):
        wait_bytes(sums.at[which, pl.ds(0, n_group - 1)], sum_recv.at[which])
        return sums[which].reshape(prefixes, sums.shape[3])

    hankel_in.start()
    own_copy(hankel, h_slab, 0).start()
    shifted_in.start()
    own_copy(shifted, s_slab, 1).start()
    begin_copy = pltpu.make_async_copy(start, begun, local_sem.at[2])
    begin_copy.start()
    barrier = pltpu.get_barrier_semaphore()

    def greet(device):
        pl.semaphore_signal(barrier, inc=1, device_id=device, device_id_type=MESH)

    loop(n_rows, lambda k: greet(in_rows(k)[1]))
    loop(n_group, lambda k: greet(in_group(k)[1]))
    pl.semaphore_wait(barrier, n_rows + n_group - 2)

    hankel_in.wait()
    send_slabs(h_own, h_slab, 0, pl.ds(0, rows_dev))
    shifted_in.wait()
    own_copy(hankel, h_slab, 0).wait()
    begin_copy.wait()
    wait_bytes(h_slab.at[pl.ds(0, n_rows - 1)], slab_recv.at[0])
    send_piece(0)
    block = split(whole(h_slab))
    scatter(split_product(block, split(begun[...])), 0)
    gram = split_product(block, block, NT)
    across(0)
    send_piece(1)
    spread(0)
    y = total(0)
    scatter(product(gram, y), 1)
    y_t = y.T
    back = split(split_product(split(y_t), block))
    across(1)
    for piece in range(2, pieces):
        send_piece(piece)
    spread(1)
    c = total(1)
    c_t = c.T

    grams = (to_tiles(product(y_t, c)), to_tiles(product(c_t, c) * (1.0 / prefixes)))
    blocks = len(grams[0])
    cuts = (5 * blocks // 16, 9 * blocks // 16, 3 * blocks // 4)
    grams = eliminate(0, cuts[0], grams)
    own_copy(shifted, s_slab, 1).wait()
    wait_bytes(s_slab.at[pl.ds(0, n_rows - 1)], slab_recv.at[1])
    scatter(split_product(split(whole(s_slab)), back, NT), 2)
    grams = eliminate(cuts[0], cuts[1], grams)
    across(2)
    grams = eliminate(cuts[1], cuts[2], grams)
    spread(2)
    right_inv, left_inv = eliminate(cuts[2], blocks, grams)
    right_inv, left_inv = from_tiles(right_inv), from_tiles(left_inv)
    mine = sums.at[1].reshape(prefixes, c.shape[1])
    basis_out[...] = product(
        mine[pl.ds(pl.multiple_of(row * rows_dev, rows_dev), rows_dev), :], left_inv, NT
    )
    crossed = product(c_t, total(2)) * (1.0 / math.sqrt(prefixes))
    operator_out[...] = product(product(left_inv, crossed), right_inv, NT)

    for which in range(2):
        wait_bytes(h_slab.at[pl.ds(0, n_rows - 1)], slab_send.at[which])
    for which in range(3):
        wait_bytes(parts.at[which, pl.ds(0, n_group - 1)], part_send.at[which])
        wait_bytes(middle.at[which, pl.ds(0, n_layers - 1)], mid_send.at[which])
        wait_bytes(sums.at[which, pl.ds(0, n_group - 1)], sum_send.at[which])


def on_device(hankel, shifted, start_basis):
    n_rows, n_cols = lax.axis_size("rows"), lax.axis_size("cols")
    near = 2
    n_group = near * n_cols
    rows_dev, cols_dev = hankel.shape
    sub, rank = cols_dev // n_rows, start_basis.shape[1]
    share = rows_dev * n_rows // n_group
    slab = pltpu.VMEM((n_rows, rows_dev, sub), jnp.float32)
    grouped = pltpu.VMEM((3, n_group, share, rank), jnp.float32)
    return pl.pallas_call(
        functools.partial(spectral_kernel, n_rows, n_cols, near),
        out_shape=[
            jax.ShapeDtypeStruct((rows_dev, rank), jnp.float32),
            jax.ShapeDtypeStruct((rank, rank), jnp.float32),
        ],
        in_specs=[pl.BlockSpec(memory_space=pltpu.HBM)] * 3,
        out_specs=[pl.BlockSpec(memory_space=pltpu.VMEM)] * 2,
        scratch_shapes=[
            pltpu.VMEM((rows_dev, cols_dev), jnp.float32),
            pltpu.VMEM((rows_dev, cols_dev), jnp.float32),
            slab,
            slab,
            pltpu.VMEM((sub, rank), jnp.float32),
            grouped,
            grouped,
            pltpu.VMEM((3, n_rows // near, share, rank), jnp.float32),
            grouped,
            pltpu.SemaphoreType.DMA((5,)),
            pltpu.SemaphoreType.DMA((2,)),
            pltpu.SemaphoreType.DMA((2,)),
        ]
        + [pltpu.SemaphoreType.DMA((3,))] * 6,
        compiler_params=pltpu.CompilerParams(
            collective_id=0, has_side_effects=True, vmem_limit_bytes=VMEM_LIMIT
        ),
    )(hankel, shifted, start_basis)


def solution(mesh):
    return jax.shard_map(
        on_device,
        mesh=mesh,
        in_specs=(P("rows", "cols"), P("rows", "cols"), P(("cols", "rows"), None)),
        out_specs=(P("rows", None), P()),
        check_vma=False,
    )
```

```python
import functools
import math

import jax
import jax.numpy as jnp
from jax import lax
from jax.experimental import pallas as pl
from jax.experimental.pallas import tpu as pltpu
from jax.sharding import PartitionSpec as P

MESH = pl.DeviceIdType.MESH
NT = (((1,), (1,)), ((), ()))
VMEM_LIMIT = 64 * 1024 * 1024 - 480 * 1024


def product(left, right, dims=(((1,), (0,)), ((), ()))):
    return lax.dot_general(
        left, right, dims, precision=lax.Precision.HIGHEST, preferred_element_type=jnp.float32
    )


def split(values):
    high = values.astype(jnp.bfloat16)
    return high, (values - high.astype(jnp.float32)).astype(jnp.bfloat16)


def split_product(left, right, dims=(((1,), (0,)), ((), ()))):
    def term(a, b):
        return lax.dot_general(a, b, dims, preferred_element_type=jnp.float32)

    return term(left[0], right[0]) + (term(left[0], right[1]) + term(left[1], right[0]))


def wait_bytes(ref, sem):
    pltpu.make_async_copy(ref, ref, sem).wait()


def eliminate(begin, end, grams):
    height, size = grams[0][0].shape
    tiles = len(grams[0])
    lane = lax.broadcasted_iota(jnp.int32, (height, size), 1)
    sublane = lax.broadcasted_iota(jnp.int32, (height, size), 0)
    line = lax.broadcasted_iota(jnp.int32, (1, size), 1)

    def block(b, held):
        held = [list(matrix) for matrix in held]
        known_from = size - height * b
        for r in range(height):
            here = lane == r
            known = (line < r) | (line >= known_from)
            for matrix in held:
                pivot = matrix[0][r : r + 1]
                diagonal = pivot[:, r : r + 1]
                inverse = 1.0 / diagonal
                scaled = jnp.broadcast_to(jnp.where(line == r, inverse, pivot * inverse), (height, size))
                final = jnp.where(known, pivot, jnp.where(line == r, 1.0, 0.0)) * lax.rsqrt(diagonal)
                for i in range(tiles - begin):
                    values = matrix[i]
                    kept = jnp.where(here, 0.0, values) - values[:, r : r + 1] * scaled
                    if i == 0:
                        kept = jnp.where(sublane > r, kept, jnp.where(sublane == r, final, values))
                    elif i > tiles - end:
                        kept = jnp.where(i < tiles - b, kept, values)
                    matrix[i] = kept
        return tuple(
            tuple(pltpu.roll(values, size - height, 1) for values in matrix[1:] + matrix[:1]) for matrix in held
        )

    return lax.fori_loop(begin, end, block, grams)


def to_tiles(gram):
    return tuple(gram[i : i + 8] for i in range(0, gram.shape[0], 8))


def from_tiles(tiles):
    return jnp.concatenate(tiles, axis=0)


def spectral_kernel(
    n_rows, n_cols, near, hankel, shifted, start, basis_out, operator_out,
    h_own, s_own, h_slab, s_slab, begun, parts, landed, middle, sums, local_sem, slab_send, slab_recv,
    part_send, part_recv, mid_send, mid_recv, sum_send, sum_recv,
):
    row, col = lax.axis_index("rows"), lax.axis_index("cols")
    layer, place = row // near, lax.rem(row, near)
    n_layers, n_group = n_rows // near, near * n_cols
    me = col * near + place
    rows_dev, sub = h_slab.shape[1:]
    prefixes = rows_dev * n_rows
    share = prefixes // n_group
    pieces = rows_dev // 8

    def loop(count, body):
        def step(k, carry):
            body(k)
            return carry

        lax.fori_loop(1, count, step, 0)

    def in_group(k):
        other = lax.rem(me + k, n_group)
        return other, {"rows": layer * near + lax.rem(other, near), "cols": other // near}

    def in_rows(k):
        other = lax.rem(row + k, n_rows)
        return other, {"rows": other, "cols": col}

    def in_layers(k):
        other = lax.rem(layer + k, n_layers)
        return other, {"rows": other * near + place, "cols": col}

    def send(source, target, sent, received, device):
        pltpu.make_async_remote_copy(
            src_ref=source,
            dst_ref=target,
            send_sem=sent,
            recv_sem=received,
            device_id=device,
            device_id_type=MESH,
        ).start()

    def own_columns(index):
        return pl.ds(pl.multiple_of(index * sub, sub), sub)

    def own_copy(source, slab, which):
        return pltpu.make_async_copy(source.at[:, own_columns(row)], slab.at[row], local_sem.at[which])

    hankel_in = pltpu.make_async_copy(hankel, h_own, local_sem.at[3])
    shifted_in = pltpu.make_async_copy(shifted, s_own, local_sem.at[4])

    def send_slabs(source, slab, which, lines):
        def body(k):
            other, device = in_rows(k)
            send(
                source.at[lines, own_columns(other)],
                slab.at[row, lines],
                slab_send.at[which],
                slab_recv.at[which],
                device,
            )

        loop(n_rows, body)

    def send_piece(piece):
        send_slabs(s_own, s_slab, 1, pl.ds(8 * piece, 8))

    def whole(slab):
        return slab[...].reshape(prefixes, sub)

    def scatter(value, which):
        parts[which] = value.reshape(n_group, share, value.shape[1])
        landed[which, 0] = parts[which, me]

        def body(k):
            other, device = in_group(k)
            send(parts.at[which, other], landed.at[which, k], part_send.at[which], part_recv.at[which], device)

        loop(n_group, body)

    def across(which):
        wait_bytes(landed.at[which, pl.ds(1, n_group - 1)], part_recv.at[which])
        middle[which, layer] = jnp.sum(landed[which], axis=0)
        mine = middle.at[which, layer]
        loop(n_layers, lambda k: send(mine, mine, mid_send.at[which], mid_recv.at[which], in_layers(k)[1]))

    def spread(which):
        wait_bytes(middle.at[which, pl.ds(0, n_layers - 1)], mid_recv.at[which])
        sums[which, me] = jnp.sum(middle[which], axis=0)
        mine = sums.at[which, me]
        loop(n_group, lambda k: send(mine, mine, sum_send.at[which], sum_recv.at[which], in_group(k)[1]))

    def total(which):
        wait_bytes(sums.at[which, pl.ds(0, n_group - 1)], sum_recv.at[which])
        return sums[which].reshape(prefixes, sums.shape[3])

    hankel_in.start()
    own_copy(hankel, h_slab, 0).start()
    shifted_in.start()
    own_copy(shifted, s_slab, 1).start()
    begin_copy = pltpu.make_async_copy(start, begun, local_sem.at[2])
    begin_copy.start()
    barrier = pltpu.get_barrier_semaphore()

    def greet(device):
        pl.semaphore_signal(barrier, inc=1, device_id=device, device_id_type=MESH)

    loop(n_rows, lambda k: greet(in_rows(k)[1]))
    loop(n_group, lambda k: greet(in_group(k)[1]))
    pl.semaphore_wait(barrier, n_rows + n_group - 2)

    hankel_in.wait()
    send_slabs(h_own, h_slab, 0, pl.ds(0, rows_dev))
    shifted_in.wait()
    own_copy(hankel, h_slab, 0).wait()
    begin_copy.wait()
    wait_bytes(h_slab.at[pl.ds(0, n_rows - 1)], slab_send.at[0])
    send_piece(0)
    wait_bytes(h_slab.at[pl.ds(0, n_rows - 1)], slab_recv.at[0])
    block = split(whole(h_slab))
    scatter(split_product(block, split(begun[...])), 0)
    gram = split_product(block, block, NT)
    across(0)
    send_piece(1)
    spread(0)
    send_piece(2)
    y = total(0)
    scatter(product(gram, y), 1)
    y_t = y.T
    back = split(split_product(split(y_t), block))
    across(1)
    for piece in range(3, pieces):
        send_piece(piece)
    spread(1)
    c = total(1)
    c_t = c.T

    grams = (to_tiles(product(y_t, c)), to_tiles(product(c_t, c) * (1.0 / prefixes)))
    blocks = len(grams[0])
    cuts = (blocks // 8, 7 * blocks // 16, 11 * blocks // 16)
    grams = eliminate(0, cuts[0], grams)
    own_copy(shifted, s_slab, 1).wait()
    wait_bytes(s_slab.at[pl.ds(0, n_rows - 1)], slab_recv.at[1])
    scatter(split_product(split(whole(s_slab)), back, NT), 2)
    grams = eliminate(cuts[0], cuts[1], grams)
    across(2)
    grams = eliminate(cuts[1], cuts[2], grams)
    spread(2)
    right_inv, left_inv = eliminate(cuts[2], blocks, grams)
    right_inv, left_inv = from_tiles(right_inv), from_tiles(left_inv)
    mine = sums.at[1].reshape(prefixes, c.shape[1])
    basis_out[...] = product(
        mine[pl.ds(pl.multiple_of(row * rows_dev, rows_dev), rows_dev), :], left_inv, NT
    )
    crossed = product(c_t, total(2)) * (1.0 / math.sqrt(prefixes))
    operator_out[...] = product(product(left_inv, crossed), right_inv, NT)

    wait_bytes(s_slab.at[pl.ds(0, n_rows - 1)], slab_send.at[1])
    for which in range(3):
        wait_bytes(parts.at[which, pl.ds(0, n_group - 1)], part_send.at[which])
        wait_bytes(middle.at[which, pl.ds(0, n_layers - 1)], mid_send.at[which])
        wait_bytes(sums.at[which, pl.ds(0, n_group - 1)], sum_send.at[which])


def on_device(hankel, shifted, start_basis):
    n_rows, n_cols = lax.axis_size("rows"), lax.axis_size("cols")
    near = 2
    n_group = near * n_cols
    rows_dev, cols_dev = hankel.shape
    sub, rank = cols_dev // n_rows, start_basis.shape[1]
    share = rows_dev * n_rows // n_group
    slab = pltpu.VMEM((n_rows, rows_dev, sub), jnp.float32)
    grouped = pltpu.VMEM((3, n_group, share, rank), jnp.float32)
    return pl.pallas_call(
        functools.partial(spectral_kernel, n_rows, n_cols, near),
        out_shape=[
            jax.ShapeDtypeStruct((rows_dev, rank), jnp.float32),
            jax.ShapeDtypeStruct((rank, rank), jnp.float32),
        ],
        in_specs=[pl.BlockSpec(memory_space=pltpu.HBM)] * 3,
        out_specs=[pl.BlockSpec(memory_space=pltpu.VMEM)] * 2,
        scratch_shapes=[
            pltpu.VMEM((rows_dev, cols_dev), jnp.float32),
            pltpu.VMEM((rows_dev, cols_dev), jnp.float32),
            slab,
            slab,
            pltpu.VMEM((sub, rank), jnp.float32),
            grouped,
            grouped,
            pltpu.VMEM((3, n_rows // near, share, rank), jnp.float32),
            grouped,
            pltpu.SemaphoreType.DMA((5,)),
            pltpu.SemaphoreType.DMA((2,)),
            pltpu.SemaphoreType.DMA((2,)),
        ]
        + [pltpu.SemaphoreType.DMA((3,))] * 6,
        compiler_params=pltpu.CompilerParams(
            collective_id=0, has_side_effects=True, vmem_limit_bytes=VMEM_LIMIT
        ),
    )(hankel, shifted, start_basis)


def solution(mesh):
    return jax.shard_map(
        on_device,
        mesh=mesh,
        in_specs=(P("rows", "cols"), P("rows", "cols"), P(("cols", "rows"), None)),
        out_specs=(P("rows", None), P()),
        check_vma=False,
    )
```

```python
import functools
import math

import jax
import jax.numpy as jnp
from jax import lax
from jax.experimental import pallas as pl
from jax.experimental.pallas import tpu as pltpu
from jax.sharding import PartitionSpec as P

MESH = pl.DeviceIdType.MESH
NT = (((1,), (1,)), ((), ()))
VMEM_LIMIT = 64 * 1024 * 1024 - 480 * 1024


def product(left, right, dims=(((1,), (0,)), ((), ()))):
    return lax.dot_general(
        left, right, dims, precision=lax.Precision.HIGHEST, preferred_element_type=jnp.float32
    )


def split(values):
    high = values.astype(jnp.bfloat16)
    return high, (values - high.astype(jnp.float32)).astype(jnp.bfloat16)


def split_product(left, right, dims=(((1,), (0,)), ((), ()))):
    def term(a, b):
        return lax.dot_general(a, b, dims, preferred_element_type=jnp.float32)

    return term(left[0], right[0]) + (term(left[0], right[1]) + term(left[1], right[0]))


def wait_bytes(ref, sem):
    pltpu.make_async_copy(ref, ref, sem).wait()


def eliminate(begin, end, grams):
    height, size = grams[0][0].shape
    tiles = len(grams[0])
    lane = lax.broadcasted_iota(jnp.int32, (height, size), 1)
    sublane = lax.broadcasted_iota(jnp.int32, (height, size), 0)
    line = lax.broadcasted_iota(jnp.int32, (1, size), 1)

    def block(b, held):
        held = [list(matrix) for matrix in held]
        known_from = size - height * b
        for r in range(height):
            here = lane == r
            known = (line < r) | (line >= known_from)
            for matrix in held:
                pivot = matrix[0][r : r + 1]
                diagonal = pivot[:, r : r + 1]
                inverse = 1.0 / diagonal
                scaled = jnp.broadcast_to(jnp.where(line == r, inverse, pivot * inverse), (height, size))
                final = jnp.where(known, pivot, jnp.where(line == r, 1.0, 0.0)) * lax.rsqrt(diagonal)
                for i in range(tiles - begin):
                    values = matrix[i]
                    kept = jnp.where(here, 0.0, values) - values[:, r : r + 1] * scaled
                    if i == 0:
                        kept = jnp.where(sublane > r, kept, jnp.where(sublane == r, final, values))
                    elif i > tiles - end:
                        kept = jnp.where(i < tiles - b, kept, values)
                    matrix[i] = kept
        return tuple(
            tuple(pltpu.roll(values, size - height, 1) for values in matrix[1:] + matrix[:1]) for matrix in held
        )

    return lax.fori_loop(begin, end, block, grams)


def to_tiles(gram):
    return tuple(gram[i : i + 8] for i in range(0, gram.shape[0], 8))


def from_tiles(tiles):
    return jnp.concatenate(tiles, axis=0)


def spectral_kernel(
    n_rows, n_cols, near, hankel, shifted, start, basis_out, operator_out,
    h_own, s_own, h_slab, s_slab, begun, parts, landed, middle, sums, local_sem, slab_send, slab_recv,
    part_send, part_recv, mid_send, mid_recv, sum_send, sum_recv,
):
    row, col = lax.axis_index("rows"), lax.axis_index("cols")
    layer, place = row // near, lax.rem(row, near)
    n_layers, n_group = n_rows // near, near * n_cols
    me = col * near + place
    rows_dev, sub = h_slab.shape[1:]
    prefixes = rows_dev * n_rows
    share = prefixes // n_group
    pieces = rows_dev // 8

    def loop(count, body):
        def step(k, carry):
            body(k)
            return carry

        lax.fori_loop(1, count, step, 0)

    def in_group(k):
        other = lax.rem(me + k, n_group)
        return other, {"rows": layer * near + lax.rem(other, near), "cols": other // near}

    def in_rows(k):
        other = lax.rem(row + k, n_rows)
        return other, {"rows": other, "cols": col}

    def in_layers(k):
        other = lax.rem(layer + k, n_layers)
        return other, {"rows": other * near + place, "cols": col}

    def send(source, target, sent, received, device):
        pltpu.make_async_remote_copy(
            src_ref=source,
            dst_ref=target,
            send_sem=sent,
            recv_sem=received,
            device_id=device,
            device_id_type=MESH,
        ).start()

    def own_columns(index):
        return pl.ds(pl.multiple_of(index * sub, sub), sub)

    def own_copy(source, slab, which):
        return pltpu.make_async_copy(source.at[:, own_columns(row)], slab.at[row], local_sem.at[which])

    hankel_in = pltpu.make_async_copy(hankel, h_own, local_sem.at[3])
    shifted_in = pltpu.make_async_copy(shifted, s_own, local_sem.at[4])

    def send_slabs(source, slab, which, lines):
        def body(k):
            other, device = in_rows(k)
            send(
                source.at[lines, own_columns(other)],
                slab.at[row, lines],
                slab_send.at[which],
                slab_recv.at[which],
                device,
            )

        loop(n_rows, body)

    def send_piece(piece):
        send_slabs(s_own, s_slab, 1, pl.ds(8 * piece, 8))

    def whole(slab):
        return slab[...].reshape(prefixes, sub)

    def scatter(value, which):
        parts[which] = value.reshape(n_group, share, value.shape[1])
        landed[which, 0] = parts[which, me]

        def body(k):
            other, device = in_group(k)
            send(parts.at[which, other], landed.at[which, k], part_send.at[which], part_recv.at[which], device)

        loop(n_group, body)

    def across(which):
        wait_bytes(landed.at[which, pl.ds(1, n_group - 1)], part_recv.at[which])
        middle[which, layer] = jnp.sum(landed[which], axis=0)
        mine = middle.at[which, layer]
        loop(n_layers, lambda k: send(mine, mine, mid_send.at[which], mid_recv.at[which], in_layers(k)[1]))

    def spread(which):
        wait_bytes(middle.at[which, pl.ds(0, n_layers - 1)], mid_recv.at[which])
        sums[which, me] = jnp.sum(middle[which], axis=0)
        mine = sums.at[which, me]
        loop(n_group, lambda k: send(mine, mine, sum_send.at[which], sum_recv.at[which], in_group(k)[1]))

    def total(which):
        wait_bytes(sums.at[which, pl.ds(0, n_group - 1)], sum_recv.at[which])
        return sums[which].reshape(prefixes, sums.shape[3])

    hankel_in.start()
    own_copy(hankel, h_slab, 0).start()
    shifted_in.start()
    own_copy(shifted, s_slab, 1).start()
    begin_copy = pltpu.make_async_copy(start, begun, local_sem.at[2])
    begin_copy.start()
    barrier = pltpu.get_barrier_semaphore()

    def greet(device):
        pl.semaphore_signal(barrier, inc=1, device_id=device, device_id_type=MESH)

    loop(n_rows, lambda k: greet(in_rows(k)[1]))
    loop(n_group, lambda k: greet(in_group(k)[1]))
    pl.semaphore_wait(barrier, n_rows + n_group - 2)

    hankel_in.wait()
    send_slabs(h_own, h_slab, 0, pl.ds(0, rows_dev))
    shifted_in.wait()
    own_copy(hankel, h_slab, 0).wait()
    begin_copy.wait()
    wait_bytes(h_slab.at[pl.ds(0, n_rows - 1)], slab_send.at[0])
    send_piece(0)
    wait_bytes(h_slab.at[pl.ds(0, n_rows - 1)], slab_recv.at[0])
    block = split(whole(h_slab))
    scatter(split_product(block, split(begun[...])), 0)
    send_piece(1)
    gram = split_product(block, block, NT)
    across(0)
    send_piece(2)
    spread(0)
    for piece in range(3, pieces):
        send_piece(piece)
    y = total(0)
    scatter(product(gram, y), 1)
    y_t = y.T
    back = split(split_product(split(y_t), block))
    across(1)
    spread(1)
    c = total(1)
    c_t = c.T

    grams = (to_tiles(product(y_t, c)), to_tiles(product(c_t, c) * (1.0 / prefixes)))
    blocks = len(grams[0])
    cuts = (blocks // 8, 7 * blocks // 16, 11 * blocks // 16)
    grams = eliminate(0, cuts[0], grams)
    own_copy(shifted, s_slab, 1).wait()
    wait_bytes(s_slab.at[pl.ds(0, n_rows - 1)], slab_recv.at[1])
    scatter(split_product(split(whole(s_slab)), back, NT), 2)
    grams = eliminate(cuts[0], cuts[1], grams)
    across(2)
    grams = eliminate(cuts[1], cuts[2], grams)
    spread(2)
    right_inv, left_inv = eliminate(cuts[2], blocks, grams)
    right_inv, left_inv = from_tiles(right_inv), from_tiles(left_inv)
    mine = sums.at[1].reshape(prefixes, c.shape[1])
    basis_out[...] = product(
        mine[pl.ds(pl.multiple_of(row * rows_dev, rows_dev), rows_dev), :], left_inv, NT
    )
    crossed = product(c_t, total(2)) * (1.0 / math.sqrt(prefixes))
    operator_out[...] = product(product(left_inv, crossed), right_inv, NT)

    wait_bytes(s_slab.at[pl.ds(0, n_rows - 1)], slab_send.at[1])
    for which in range(3):
        wait_bytes(parts.at[which, pl.ds(0, n_group - 1)], part_send.at[which])
        wait_bytes(middle.at[which, pl.ds(0, n_layers - 1)], mid_send.at[which])
        wait_bytes(sums.at[which, pl.ds(0, n_group - 1)], sum_send.at[which])


def on_device(hankel, shifted, start_basis):
    n_rows, n_cols = lax.axis_size("rows"), lax.axis_size("cols")
    near = 2
    n_group = near * n_cols
    rows_dev, cols_dev = hankel.shape
    sub, rank = cols_dev // n_rows, start_basis.shape[1]
    share = rows_dev * n_rows // n_group
    slab = pltpu.VMEM((n_rows, rows_dev, sub), jnp.float32)
    grouped = pltpu.VMEM((3, n_group, share, rank), jnp.float32)
    return pl.pallas_call(
        functools.partial(spectral_kernel, n_rows, n_cols, near),
        out_shape=[
            jax.ShapeDtypeStruct((rows_dev, rank), jnp.float32),
            jax.ShapeDtypeStruct((rank, rank), jnp.float32),
        ],
        in_specs=[pl.BlockSpec(memory_space=pltpu.HBM)] * 3,
        out_specs=[pl.BlockSpec(memory_space=pltpu.VMEM)] * 2,
        scratch_shapes=[
            pltpu.VMEM((rows_dev, cols_dev), jnp.float32),
            pltpu.VMEM((rows_dev, cols_dev), jnp.float32),
            slab,
            slab,
            pltpu.VMEM((sub, rank), jnp.float32),
            grouped,
            grouped,
            pltpu.VMEM((3, n_rows // near, share, rank), jnp.float32),
            grouped,
            pltpu.SemaphoreType.DMA((5,)),
            pltpu.SemaphoreType.DMA((2,)),
            pltpu.SemaphoreType.DMA((2,)),
        ]
        + [pltpu.SemaphoreType.DMA((3,))] * 6,
        compiler_params=pltpu.CompilerParams(
            collective_id=0, has_side_effects=True, vmem_limit_bytes=VMEM_LIMIT
        ),
    )(hankel, shifted, start_basis)


def solution(mesh):
    return jax.shard_map(
        on_device,
        mesh=mesh,
        in_specs=(P("rows", "cols"), P("rows", "cols"), P(("cols", "rows"), None)),
        out_specs=(P("rows", None), P()),
        check_vma=False,
    )
```
